768 devices in a mesh: row: 32 (over z_hi, x, core), col: 24 (over z_lo, y).
Axes of the slice: x: 4, y: 8, z: 12 (z_hi: 4, z_lo: 3; z = z_hi * 3 + z_lo), core: 2. Of those that a mesh axis runs over, the one named last changes fastest.
Arguments:
- u_blocks: float32 [96, 168, 128, 128], P('row', 'col'), may hold values from -0.21875 to 0.21875
- u_rows: int32 [96, 168], P('row', 'col'), may hold values from 0 to 2
Outputs:
- squares: float32 [128, 72, 3, 128, 128], P('row', 'col')
The draws below stay inside these ranges and needn't reach their ends.
All inputs are finite; a program needn't handle non-finite values.
Results may differ from the reference program's by a relative error of at most 0.0001.
Values sent between devices are 32-bit elements; how exact they have to be, the bound alone decides.
A program may use at most 32 MiB of HBM per device.

```python
import jax
import jax.numpy as jnp
from jax import lax

BS = 128
TAU = 3
DIRS = 7
STEPS = 4
N_ROW = 32
N_COL = 24


def set_ends(entries, own_key, least, top_value):
    spot = [jax.random.randint(jax.random.fold_in(own_key, axis), (), 0, length) for axis, length in enumerate(entries.shape)]
    widest = entries.shape.index(max(entries.shape))
    neighbour = spot[:widest] + [(spot[widest] + 1) % entries.shape[widest]] + spot[widest + 1:]
    return entries.at[tuple(spot)].set(least).at[tuple(neighbour)].set(top_value)


def level_of(rng, shape, shards, low, largest):
    gain, own = 1.0, jax.random.fold_in(rng, 6)
    for axis_at, parts in shards:
        steps = jnp.exp(jax.random.uniform(jax.random.fold_in(own, axis_at), (parts,), jnp.float32, low / len(shards), largest / len(shards)))
        gain = gain * jnp.repeat(steps, shape[axis_at] // parts).reshape([-1 if axis == axis_at else 1 for axis in range(len(shape))])
    return gain


def noise(own_key, extent, deviation, reach, cuts=(), held_as=jnp.bfloat16):
    gain = level_of(own_key, extent, cuts, -0.22, 0.18) if cuts else 1.0
    drawn = jax.random.normal(own_key, extent, jnp.float32) * deviation * gain
    return jnp.minimum(jnp.maximum(drawn, -reach), reach).astype(held_as)


def setup_inputs(seed: int = 0) -> dict:
    streams_of = jax.random.split(jax.random.key(seed), 3)
    return {
        "u_blocks": noise(streams_of[0], (N_ROW * TAU, N_COL * DIRS, BS, BS), (2 * TAU * BS) ** -0.5, 0.21875, ((0, 32), (1, 24)), jnp.float32),
        "u_rows": set_ends(jax.random.randint(streams_of[1], (N_ROW * TAU, N_COL * DIRS), 0, TAU), jax.random.fold_in(streams_of[1], 1), 0, TAU - 1).astype(jnp.int32),
    }


def one_hot(rows, count):
    return (rows[..., None] == jnp.arange(count, dtype=jnp.int32)).astype(jnp.float32)


def place_columns(hot_rows, blocks):
    return jnp.einsum("...ki,...kab->...ikab", hot_rows, blocks, precision=lax.Precision.HIGHEST)


def place_transposed(hot_rows, blocks):
    return jnp.einsum("...ik,...iba->...ikab", hot_rows, blocks, precision=lax.Precision.HIGHEST)


def block_product(left_side, right_side):
    return jnp.einsum("...ikab,...kjbc->...ijac", left_side, right_side, precision=lax.Precision.HIGHEST)


def rolled(field, first, second):
    return jnp.roll(field, (-first, -second), axis=(0, 1))


def reference(u_blocks, u_rows):
    width = u_blocks.shape[-1]
    blocks = u_blocks.reshape(N_ROW, TAU, N_COL, DIRS, width, width).transpose(0, 2, 1, 3, 4, 5)
    labels = u_rows.reshape(N_ROW, TAU, N_COL, DIRS).transpose(0, 2, 1, 3)
    onsite_hot = one_hot(labels[:, :, :, 0], TAU)
    onsite = place_columns(onsite_hot, blocks[:, :, :, 0]) + place_transposed(onsite_hot, blocks[:, :, :, 0])
    results = [block_product(onsite, onsite)]
    for step in range(1, STEPS):
        forward = blocks[:, :, :, step]
        backward = blocks[:, :, :, step + STEPS - 1]
        forward_hot = one_hot(labels[:, :, :, step], TAU)
        backward_hot = one_hot(labels[:, :, :, step + STEPS - 1], TAU)
        left_side = place_columns(rolled(forward_hot, step, step), rolled(forward, step, step))
        left_side = left_side + place_transposed(rolled(backward_hot, 0, 2 * step), rolled(backward, 0, 2 * step))
        right_side = place_columns(rolled(forward_hot, 2 * step, 0), rolled(forward, 2 * step, 0))
        right_side = right_side + place_transposed(rolled(backward_hot, step, step), rolled(backward, step, step))
        results.append(block_product(left_side, right_side))
    stacked = jnp.stack(results, axis=2)
    stacked = stacked.transpose(0, 2, 1, 3, 4, 5, 6)
    return stacked.reshape(N_ROW * STEPS, N_COL * TAU, TAU, width, width)
```

```python
import functools

import jax
import jax.numpy as jnp
from jax import lax
from jax.experimental import pallas as pl
from jax.experimental.pallas import tpu as pltpu
from jax.sharding import PartitionSpec as P

MESH = pl.DeviceIdType.MESH
BS = 128
TAU = 3
STEPS = 4
N_ROW = 32
N_COL = 24
HEIGHT = TAU * BS + 8

RING = 8


def straight(k, m):
    return (
        lambda r, c: ((r + N_ROW - k) % N_ROW, (c + N_COL - m) % N_COL),
        lambda r, c: ((r + N_ROW + k) % N_ROW, (c + N_COL + m) % N_COL),
    )


def around(at, k):
    return at - at % RING + (at % RING + RING - k) % RING


def in_plane(k, m):
    return lambda r, c: (around(r, k), around(c, m)), lambda r, c: (around(r, -k), around(c, -m))


def in_row_plane(k, m):
    return (
        lambda r, c: (around(r, k), (c + N_COL - m) % N_COL),
        lambda r, c: (around(r, -k), (c + m) % N_COL),
    )


def wrapped(at, k):
    return jnp.where(at % RING >= RING - k, RING, 0)


def down(k, m):
    return (
        lambda r, c: ((r + N_ROW - wrapped(r, k)) % N_ROW, (c + N_COL - wrapped(c, m)) % N_COL),
        lambda r, c: ((r + wrapped(r, k)) % N_ROW, (c + wrapped(c, m)) % N_COL),
    )


class Leg:
    def __init__(self, name, src, move, sends=None):
        self.name, self.src, self.sends = name, src, sends
        self.to, self.origin = move
        self.gets = None if sends is None else lambda r, c: sends(*self.origin(r, c))


def plan():
    legs, final = [], {}

    def late(name, src, k, m):
        crossed = lambda r, c: (r % RING >= RING - k) | (c % RING >= RING - m)
        legs.append(Leg(name, src, in_plane(k, m)))
        return Leg(name + "z", name, down(k, m), crossed), (crossed, name + "z", name)

    def shared(s):
        low = lambda k: lambda r, c: r % RING < k
        legs.append(Leg(f"f{s}", f"F{s}", straight(RING, 0), low(2 * s)))
        return [
            Leg(f"fe{s}", (low(2 * s), f"f{s}", f"F{s}"), in_plane(2 * s, 0)),
            Leg(f"fm{s}", (low(s), f"f{s}", f"F{s}"), in_row_plane(s, s)),
        ]

    f3 = shared(3)
    f2 = shared(2)
    bm2, bm2_at = late("bm2", "B2", 2, 2)
    bs2, bs2_at = late("bs2", "B2", 0, 4)
    fe1, fe1_at = late("fe1", "F1", 2, 0)
    fm1, fm1_at = late("fm1", "F1", 1, 1)
    bm1, bm1_at = late("bm1", "B1", 1, 1)
    legs += [Leg("bs3", "B3", straight(0, 6)), Leg("bs1", "B1", straight(0, 2))]
    legs += [fe1, fm1, bm1, bm2, bs2] + f2 + f3 + [Leg("bm3", "bs3", straight(3, -3))]
    final[1] = fm1_at, "bs1", fe1_at, bm1_at
    final[2] = "fm2", bs2_at, "fe2", bm2_at
    final[3] = "fm3", "bs3", "fe3", "bm3"
    return legs, final


OWN = ["F1", "F2", "F3", "B1", "B2", "B3"]


def places(legs):
    return {name: at for at, name in enumerate(OWN + [leg.name for leg in legs])}


def pick(src, at, r, c):
    if isinstance(src, str):
        return at[src]
    condition, yes, no = src
    return jnp.where(condition(r, c), at[yes], at[no])


def names(src):
    return {src} if isinstance(src, str) else set(src[1:])


def when(condition, r, c, do):
    if condition is None:
        do()
    else:
        pl.when(condition(r, c))(do)


def split(value):
    high = value.astype(jnp.bfloat16)
    return high, (value - high.astype(jnp.float32)).astype(jnp.bfloat16)


def dot(a, b):
    return jnp.dot(a, b, preferred_element_type=jnp.float32)


def kernel(legs, final, u_ref, rows_ref, out_ref, buf, onsite, lefts, rights, result, load_sem, store_sem, send_sem, recv_sem):
    r, c = lax.axis_index("row"), lax.axis_index("col")
    at = places(legs)
    copies = {}
    for number, leg in enumerate(legs):
        copies[leg.name] = pltpu.make_async_remote_copy(
            src_ref=buf.at[pick(leg.src, at, r, c)],
            dst_ref=buf.at[at[leg.name]],
            send_sem=send_sem.at[number],
            recv_sem=recv_sem.at[number],
            device_id=leg.to(r, c),
            device_id_type=MESH,
        )

    barrier = pltpu.get_barrier_semaphore()
    partners = 0
    for leg in legs:
        greet = functools.partial(
            pl.semaphore_signal, barrier, inc=1, device_id=leg.origin(r, c), device_id_type=MESH
        )
        when(leg.gets, r, c, greet)
        partners += 1 if leg.sends is None else jnp.where(leg.sends(r, c), 1, 0)

    loads = []
    for j in range(2 * STEPS - 1):
        for t in range(TAU):
            target = onsite.at[t] if j == 0 else buf.at[j - 1, pl.ds(t * BS, BS)]
            loads.append(pltpu.make_async_copy(u_ref.at[t, j], target, load_sem.at[j, t]))
            loads[-1].start()
    for j in range(1, 2 * STEPS - 1):
        label = jnp.concatenate(
            [jnp.full((1, BS), rows_ref[t, j], jnp.int32) for t in range(TAU)] + [jnp.zeros((8 - TAU, BS), jnp.int32)]
        )
        buf[j - 1, TAU * BS : HEIGHT, :] = label.astype(jnp.float32)
    for load in loads:
        load.wait()
    pl.semaphore_wait(barrier, partners)

    for leg in legs:
        if leg.src in OWN:
            when(leg.sends, r, c, copies[leg.name].start)
        elif not isinstance(leg.src, str) and leg.src[2] in OWN:
            when(lambda r, c: jnp.logical_not(leg.src[0](r, c)), r, c, copies[leg.name].start)

    def put(side, i, k, value):
        high, low = split(value)
        side[0, i * BS : (i + 1) * BS, k * BS : (k + 1) * BS] = high
        side[1, i * BS : (i + 1) * BS, k * BS : (k + 1) * BS] = low

    def chosen(label, k, block):
        return jnp.where(label == float(k), block, 0.0)

    def assemble(side, forward, forward_labels, backward, backward_labels):
        for i in range(TAU):
            turned = backward(i).T
            for k in range(TAU):
                put(side, i, k, chosen(forward_labels(k), i, forward(k)) + chosen(backward_labels(i), k, turned))

    def multiply(s, left, right):
        for i in range(TAU):
            rows = slice(i * BS, (i + 1) * BS)
            high = left[0, rows, :]
            total = dot(high, right[1]) + dot(left[1, rows, :], right[0]) + dot(high, right[0])
            for j in range(TAU):
                result[s, i, j] = total[:, j * BS : (j + 1) * BS]
        store = pltpu.make_async_copy(result.at[s], out_ref.at[s], store_sem.at[s])
        store.start()
        return store

    own_labels = lambda t: jnp.full((1, BS), rows_ref[t, 0], jnp.int32).astype(jnp.float32)
    own_block = lambda t: onsite[t]
    assemble(lefts, own_block, own_labels, own_block, own_labels)
    stores = [multiply(0, lefts, lefts)]

    def parts_of(src):
        place = pick(src, at, r, c)
        block = lambda t: buf[place, t * BS : (t + 1) * BS, :]
        labels = lambda t: buf[place, TAU * BS + t : TAU * BS + t + 1, :]
        return block, labels

    arrived = set(OWN)
    for leg in legs:
        when(leg.gets, r, c, copies[leg.name].wait_recv)
        arrived.add(leg.name)
        for later in legs:
            if leg.name in names(later.src):
                if isinstance(later.src, str):
                    when(later.sends, r, c, copies[later.name].start)
                else:
                    when(later.src[0], r, c, copies[later.name].start)
        for s in range(1, STEPS):
            needs = set().union(*(names(src) for src in final[s]))
            if leg.name in needs and arrived >= needs:
                fm, bs, fe, bm = (parts_of(src) for src in final[s])
                assemble(lefts, *fm, *bs)
                assemble(rights, *fe, *bm)
                stores.append(multiply(s, lefts, rights))
    for leg in legs:
        when(leg.sends, r, c, copies[leg.name].wait_send)
    for store in stores:
        store.wait()


def shards(u_blocks, u_rows):
    legs, final = plan()
    count = len(OWN) + len(legs)
    return pl.pallas_call(
        functools.partial(kernel, legs, final),
        out_shape=jax.ShapeDtypeStruct((STEPS, TAU, TAU, BS, BS), jnp.float32),
        in_specs=[pl.BlockSpec(memory_space=pl.ANY), pl.BlockSpec(memory_space=pltpu.SMEM)],
        out_specs=pl.BlockSpec(memory_space=pl.ANY),
        scratch_shapes=[
            pltpu.VMEM((count, HEIGHT, BS), jnp.float32),
            pltpu.VMEM((TAU, BS, BS), jnp.float32),
            pltpu.VMEM((2, TAU * BS, TAU * BS), jnp.bfloat16),
            pltpu.VMEM((2, TAU * BS, TAU * BS), jnp.bfloat16),
            pltpu.VMEM((STEPS, TAU, TAU, BS, BS), jnp.float32),
            pltpu.SemaphoreType.DMA((2 * STEPS - 1, TAU)),
            pltpu.SemaphoreType.DMA((STEPS,)),
            pltpu.SemaphoreType.DMA((len(legs),)),
            pltpu.SemaphoreType.DMA((len(legs),)),
        ],
        compiler_params=pltpu.CompilerParams(collective_id=0, has_side_effects=True, vmem_limit_bytes=48 << 20),
    )(u_blocks, u_rows)


def solution(mesh):
    return jax.shard_map(
        shards,
        mesh=mesh,
        in_specs=(P("row", "col", None, None), P("row", "col")),
        out_specs=P("row", "col", None, None, None),
        check_vma=False,
    )
```

```python
import functools

import jax
import jax.numpy as jnp
from jax import lax
from jax.experimental import pallas as pl
from jax.experimental.pallas import tpu as pltpu
from jax.sharding import PartitionSpec as P

MESH = pl.DeviceIdType.MESH
BS = 128
TAU = 3
STEPS = 4
N_ROW = 32
N_COL = 24
HEIGHT = BS + 8

RING = 8


def straight(k, m):
    return (
        lambda r, c: ((r + N_ROW - k) % N_ROW, (c + N_COL - m) % N_COL),
        lambda r, c: ((r + N_ROW + k) % N_ROW, (c + N_COL + m) % N_COL),
    )


def around(at, k):
    return at - at % RING + (at % RING + RING - k) % RING


def in_plane(k, m):
    return lambda r, c: (around(r, k), around(c, m)), lambda r, c: (around(r, -k), around(c, -m))


def in_row_plane(k, m):
    return (
        lambda r, c: (around(r, k), (c + N_COL - m) % N_COL),
        lambda r, c: (around(r, -k), (c + m) % N_COL),
    )


def wrapped(at, k):
    return jnp.where(at % RING >= RING - k, RING, 0)


def down(k, m):
    return (
        lambda r, c: ((r + N_ROW - wrapped(r, k)) % N_ROW, (c + N_COL - wrapped(c, m)) % N_COL),
        lambda r, c: ((r + wrapped(r, k)) % N_ROW, (c + wrapped(c, m)) % N_COL),
    )


class Leg:
    def __init__(self, name, src, move, sends=None):
        self.name, self.src, self.sends, self.after = name, src, sends, AFTER.get(name)
        self.to, self.origin = move
        self.gets = None if sends is None else lambda r, c: sends(*self.origin(r, c))


def plan():
    legs, final = {}, {}

    def leg(name, src, move, sends=None):
        legs[name] = Leg(name, src, move, sends)
        return name

    def late(name, src, k, m):
        crossed = lambda r, c: (r % RING >= RING - k) | (c % RING >= RING - m)
        leg(name, src, in_plane(k, m))
        leg(name + "z", name, down(k, m), crossed)
        return crossed, name + "z", name

    low = lambda k: lambda r, c: r % RING < k
    rows = lambda a, b: lambda r, c: (r % RING >= a) & (r % RING < b)
    wide = lambda r, c: c % RING >= 4

    leg("f3", "F3", straight(RING, 0), low(6))
    leg("fe3", (low(6), "f3", "F3"), in_plane(6, 0))
    leg("fm3", (low(3), "f3", "F3"), in_row_plane(3, 3))
    bs3 = late("bs3", "B3", 0, 6)
    leg("bm3", bs3, straight(3, -3))
    final[3] = "fm3", bs3, "fe3", "bm3"

    leg("f2", "F2", straight(RING, 0), rows(2, 4))
    leg("fe2", (rows(2, 4), "f2", "F2"), in_plane(4, 0))
    leg("fe2z", "fe2", straight(RING, 0), rows(4, 6))
    leg("fm2", "F2", in_row_plane(2, 2), rows(2, 8))
    leg("fm2x", "fe2z", in_row_plane(-2, 2), rows(4, 6))
    leg("p2", "B2", in_plane(0, -2))
    leg("bs2", "p2", in_plane(0, -2))
    leg("bs2z", "bs2", down(0, 4), wide)
    bm2 = late("bm2", "B2", 2, 2)
    final[2] = (rows(6, 8), "fm2x", "fm2"), (wide, "bs2z", "bs2"), (rows(4, 6), "fe2z", "fe2"), bm2

    n1 = late("n1", "F1", 1, 0)
    c1 = leg("c1", "B1", straight(0, 1))
    fe1 = late("fe1", n1, 1, 0)
    fm1 = late("fm1", n1, 0, 1)
    leg("bm1", c1, straight(1, 0))
    leg("bs1", c1, straight(0, 1))
    final[1] = fm1, "bs1", fe1, "bm1"

    return [legs[name] for name in ORDER], final


ORDER = (
    "n1", "n1z", "p2", "fe1", "fe1z", "f3", "f2", "bs3", "fm1", "bs3z", "fe2", "fe2z", "bm2", "c1", "bs2", "fe3",
    "bm1", "fm3", "bs1", "fm2", "fm2x", "bm3", "fm1z", "bm2z", "bs2z",
)
AFTER = {"bm2": "n1", "c1": "bs3", "f2": "n1", "f3": "n1", "fe2": "n1", "fm3": "f2", "p2": "n1"}


OWN = ["F1", "F2", "F3", "B1", "B2", "B3"]


def places(legs):
    return {name: at for at, name in enumerate(OWN + [leg.name for leg in legs])}


def pick(src, at, r, c):
    if isinstance(src, str):
        return at[src]
    condition, yes, no = src
    return jnp.where(condition(r, c), at[yes], at[no])


def names(src):
    return {src} if isinstance(src, str) else set(src[1:])


def when(condition, r, c, do):
    if condition is None:
        do()
    else:
        pl.when(condition(r, c))(do)


def split(value):
    high = value.astype(jnp.bfloat16)
    return high, (value - high.astype(jnp.float32)).astype(jnp.bfloat16)


def dot(a, b):
    return jnp.dot(a, b, preferred_element_type=jnp.float32)


def kernel(legs, final, u_ref, rows_hbm, out_ref, buf, onsite, rows_ref, lefts, rights, result, rows_sem, load_sem, store_sem, send_sem, recv_sem):
    r, c = lax.axis_index("row"), lax.axis_index("col")
    at = places(legs)
    copies = {}
    for number, leg in enumerate(legs):
        copies[leg.name] = pltpu.make_async_remote_copy(
            src_ref=buf.at[pick(leg.src, at, r, c)],
            dst_ref=buf.at[at[leg.name]],
            send_sem=send_sem.at[number],
            recv_sem=recv_sem.at[number],
            device_id=leg.to(r, c),
            device_id_type=MESH,
        )

    barrier = pltpu.get_barrier_semaphore()
    partners = 0
    for leg in legs:
        greet = functools.partial(
            pl.semaphore_signal, barrier, inc=1, device_id=leg.origin(r, c), device_id_type=MESH
        )
        when(leg.gets, r, c, greet)
        partners += 1 if leg.sends is None else jnp.where(leg.sends(r, c), 1, 0)

    loads = [pltpu.make_async_copy(rows_hbm, rows_ref, rows_sem)]
    loads[0].start()
    for j in range(2 * STEPS - 1):
        for t in range(TAU):
            target = onsite.at[t] if j == 0 else buf.at[j - 1, t, pl.ds(0, BS)]
            loads.append(pltpu.make_async_copy(u_ref.at[t, j], target, load_sem.at[j, t]))
            loads[-1].start()
    loads[0].wait()
    for j in range(1, 2 * STEPS - 1):
        for t in range(TAU):
            buf[j - 1, t, BS:HEIGHT, :] = jnp.full((HEIGHT - BS, BS), rows_ref[t, j], jnp.int32).astype(jnp.float32)
    for load in loads[1:]:
        load.wait()
    pl.semaphore_wait(barrier, partners)

    def begin(event):
        for leg in legs:
            go = copies[leg.name].start
            if isinstance(leg.src, str):
                if event == (leg.after if leg.src in OWN else leg.src):
                    when(leg.sends, r, c, go)
            else:
                condition, yes, no = leg.src
                if event == yes:
                    when(condition, r, c, go)
                if event == (leg.after if no in OWN else no):
                    when(lambda r, c: jnp.logical_not(condition(r, c)), r, c, go)

    begin(None)

    def put(side, i, k, value):
        high, low = split(value)
        side[0, i * BS : (i + 1) * BS, k * BS : (k + 1) * BS] = high
        side[1, i * BS : (i + 1) * BS, k * BS : (k + 1) * BS] = low

    def chosen(label, k, block):
        return jnp.where(label == float(k), block, 0.0)

    def assemble(side, forward, forward_labels, backward, backward_labels):
        for i in range(TAU):
            turned = backward(i).T
            for k in range(TAU):
                put(side, i, k, chosen(forward_labels(k), i, forward(k)) + chosen(backward_labels(i), k, turned))

    def multiply(s, left, right):
        for i in range(TAU):
            rows = slice(i * BS, (i + 1) * BS)
            high = left[0, rows, :]
            total = dot(high, right[1]) + dot(left[1, rows, :], right[0]) + dot(high, right[0])
            for j in range(TAU):
                result[s, i, j] = total[:, j * BS : (j + 1) * BS]
        store = pltpu.make_async_copy(result.at[s], out_ref.at[s], store_sem.at[s])
        store.start()
        return store

    own_labels = lambda t: jnp.full((1, BS), rows_ref[t, 0], jnp.int32).astype(jnp.float32)
    own_block = lambda t: onsite[t]
    assemble(lefts, own_block, own_labels, own_block, own_labels)
    stores = [multiply(0, lefts, lefts)]

    def parts_of(src):
        place = pick(src, at, r, c)
        block = lambda t: buf[place, t, :BS, :]
        labels = lambda t: buf[place, t, BS : BS + 1, :]
        return block, labels

    arrived = set(OWN)
    for leg in legs:
        when(leg.gets, r, c, copies[leg.name].wait_recv)
        arrived.add(leg.name)
        begin(leg.name)
        for s in range(1, STEPS):
            needs = set().union(*(names(src) for src in final[s]))
            if leg.name in needs and arrived >= needs:
                fm, bs, fe, bm = (parts_of(src) for src in final[s])
                assemble(lefts, *fm, *bs)
                assemble(rights, *fe, *bm)
                stores.append(multiply(s, lefts, rights))
    for leg in legs:
        when(leg.sends, r, c, copies[leg.name].wait_send)
    for store in stores:
        store.wait()


def shards(u_blocks, u_rows):
    legs, final = plan()
    count = len(OWN) + len(legs)
    return pl.pallas_call(
        functools.partial(kernel, legs, final),
        out_shape=jax.ShapeDtypeStruct((STEPS, TAU, TAU, BS, BS), jnp.float32),
        in_specs=[pl.BlockSpec(memory_space=pltpu.HBM)] * 2,
        out_specs=pl.BlockSpec(memory_space=pl.ANY),
        scratch_shapes=[
            pltpu.VMEM((count, TAU, HEIGHT, BS), jnp.float32),
            pltpu.VMEM((TAU, BS, BS), jnp.float32),
            pltpu.SMEM((TAU, 2 * STEPS - 1), jnp.int32),
            pltpu.VMEM((2, TAU * BS, TAU * BS), jnp.bfloat16),
            pltpu.VMEM((2, TAU * BS, TAU * BS), jnp.bfloat16),
            pltpu.VMEM((STEPS, TAU, TAU, BS, BS), jnp.float32),
            pltpu.SemaphoreType.DMA,
            pltpu.SemaphoreType.DMA((2 * STEPS - 1, TAU)),
            pltpu.SemaphoreType.DMA((STEPS,)),
            pltpu.SemaphoreType.DMA((len(legs),)),
            pltpu.SemaphoreType.DMA((len(legs),)),
        ],
        compiler_params=pltpu.CompilerParams(collective_id=0, has_side_effects=True, vmem_limit_bytes=48 << 20),
    )(u_blocks, u_rows)


def solution(mesh):
    return jax.shard_map(
        shards,
        mesh=mesh,
        in_specs=(P("row", "col", None, None), P("row", "col")),
        out_specs=P("row", "col", None, None, None),
        check_vma=False,
    )
```

```python
import functools

import jax
import jax.numpy as jnp
from jax import lax
from jax.experimental import pallas as pl
from jax.experimental.pallas import tpu as pltpu
from jax.sharding import PartitionSpec as P

MESH = pl.DeviceIdType.MESH
BS = 128
TAU = 3
STEPS = 4
N_ROW = 32
N_COL = 24
HEIGHT = BS + 8

RING = 8


def straight(k, m):
    return (
        lambda r, c: ((r + N_ROW - k) % N_ROW, (c + N_COL - m) % N_COL),
        lambda r, c: ((r + N_ROW + k) % N_ROW, (c + N_COL + m) % N_COL),
    )


def around(at, k):
    return at - at % RING + (at % RING + RING - k) % RING


def in_plane(k, m):
    return lambda r, c: (around(r, k), around(c, m)), lambda r, c: (around(r, -k), around(c, -m))


def in_row_plane(k, m):
    return (
        lambda r, c: (around(r, k), (c + N_COL - m) % N_COL),
        lambda r, c: (around(r, -k), (c + m) % N_COL),
    )


def wrapped(at, k):
    return jnp.where(at % RING >= RING - k, RING, 0)


def down(k, m):
    return (
        lambda r, c: ((r + N_ROW - wrapped(r, k)) % N_ROW, (c + N_COL - wrapped(c, m)) % N_COL),
        lambda r, c: ((r + wrapped(r, k)) % N_ROW, (c + wrapped(c, m)) % N_COL),
    )


class Leg:
    def __init__(self, name, src, move, sends=None):
        self.name, self.src, self.sends, self.after = name, src, sends, AFTER.get(name)
        self.to, self.origin = move
        self.gets = None if sends is None else lambda r, c: sends(*self.origin(r, c))


def plan():
    legs, final = {}, {}

    def leg(name, src, move, sends=None):
        legs[name] = Leg(name, src, move, sends)
        return name

    def late(name, src, k, m):
        crossed = lambda r, c: (r % RING >= RING - k) | (c % RING >= RING - m)
        leg(name, src, in_plane(k, m))
        leg(name + "z", name, down(k, m), crossed)
        return crossed, name + "z", name

    low = lambda k: lambda r, c: r % RING < k
    rows = lambda a, b: lambda r, c: (r % RING >= a) & (r % RING < b)
    wide = lambda r, c: c % RING >= 4

    leg("f3", "F3", straight(RING, 0), low(6))
    leg("fe3", (low(6), "f3", "F3"), in_plane(6, 0))
    leg("fm3", (low(3), "f3", "F3"), in_row_plane(3, 3))
    bs3 = leg("bs3", "B3", straight(0, 6))
    leg("bm3", bs3, straight(3, -3))
    final[3] = "fm3", bs3, "fe3", "bm3"

    leg("f2", "F2", straight(RING, 0), rows(2, 4))
    leg("fe2", (rows(2, 4), "f2", "F2"), in_plane(4, 0))
    leg("fe2z", "fe2", straight(RING, 0), rows(4, 6))
    leg("fm2", "F2", in_row_plane(2, 2), rows(2, 8))
    leg("fm2x", "fe2z", in_row_plane(-2, 2), rows(4, 6))
    leg("p2", "B2", in_plane(0, -2))
    leg("bs2", "p2", in_plane(0, -2))
    leg("bs2z", "bs2", down(0, 4), wide)
    bm2 = late("bm2", "B2", 2, 2)
    final[2] = (rows(6, 8), "fm2x", "fm2"), (wide, "bs2z", "bs2"), (rows(4, 6), "fe2z", "fe2"), bm2

    n1 = late("n1", "F1", 1, 0)
    c1 = leg("c1", "B1", straight(0, 1))
    fe1 = late("fe1", n1, 1, 0)
    fm1 = late("fm1", n1, 0, 1)
    leg("bm1", c1, straight(1, 0))
    leg("bs1", c1, straight(0, 1))
    final[1] = fm1, "bs1", fe1, "bm1"

    return [legs[name] for name in ORDER], final


ORDER = (
    "n1", "n1z", "fe1", "p2", "f3", "f2", "bs3", "fe1z", "fm1", "fe2", "fe2z", "fe3", "bm2", "c1", "bs2", "bm1",
    "fm3", "bm2z", "fm1z", "bs1", "fm2", "fm2x", "bs2z", "bm3",
)
AFTER = {"bm2": "n1", "c1": "f2", "fe2": "fe1", "fm3": "f2", "p2": "n1"}


OWN = ["F1", "F2", "F3", "B1", "B2", "B3"]


def places(legs):
    return {name: at for at, name in enumerate(OWN + [leg.name for leg in legs])}


def pick(src, at, r, c):
    if isinstance(src, str):
        return at[src]
    condition, yes, no = src
    return jnp.where(condition(r, c), at[yes], at[no])


def names(src):
    return {src} if isinstance(src, str) else set(src[1:])


def when(condition, r, c, do):
    if condition is None:
        do()
    else:
        pl.when(condition(r, c))(do)


def split(value):
    high = value.astype(jnp.bfloat16)
    return high, (value - high.astype(jnp.float32)).astype(jnp.bfloat16)


def dot(a, b):
    return jnp.dot(a, b, preferred_element_type=jnp.float32)


def kernel(legs, final, u_ref, rows_hbm, out_ref, buf, onsite, rows_ref, sides, rows_sem, load_sem, send_sem, recv_sem):
    r, c = lax.axis_index("row"), lax.axis_index("col")
    at = places(legs)
    copies = {}
    for number, leg in enumerate(legs):
        copies[leg.name] = pltpu.make_async_remote_copy(
            src_ref=buf.at[pick(leg.src, at, r, c)],
            dst_ref=buf.at[at[leg.name]],
            send_sem=send_sem.at[number],
            recv_sem=recv_sem.at[number],
            device_id=leg.to(r, c),
            device_id_type=MESH,
        )

    barrier = pltpu.get_barrier_semaphore()
    partners = 0
    for leg in legs:
        greet = functools.partial(
            pl.semaphore_signal, barrier, inc=1, device_id=leg.origin(r, c), device_id_type=MESH
        )
        when(leg.gets, r, c, greet)
        partners += 1 if leg.sends is None else jnp.where(leg.sends(r, c), 1, 0)

    loads = [pltpu.make_async_copy(rows_hbm, rows_ref, rows_sem)]
    loads[0].start()
    for j in range(2 * STEPS - 1):
        for t in range(TAU):
            target = onsite.at[t] if j == 0 else buf.at[j - 1, t, pl.ds(0, BS)]
            loads.append(pltpu.make_async_copy(u_ref.at[t, j], target, load_sem.at[j, t]))
            loads[-1].start()
    loads[0].wait()
    for j in range(1, 2 * STEPS - 1):
        for t in range(TAU):
            buf[j - 1, t, BS:HEIGHT, :] = jnp.full((HEIGHT - BS, BS), rows_ref[t, j], jnp.int32).astype(jnp.float32)
    for load in loads[1:]:
        load.wait()
    pl.semaphore_wait(barrier, partners)

    rank = {None: -1, **{leg.name: number for number, leg in enumerate(legs)}}

    def trigger(leg, source):
        return max(None if source in OWN else source, leg.after, key=rank.get)

    def begin(event):
        for leg in legs:
            go = copies[leg.name].start
            if isinstance(leg.src, str):
                if event == trigger(leg, leg.src):
                    when(leg.sends, r, c, go)
            else:
                condition, yes, no = leg.src
                if event == trigger(leg, yes):
                    when(condition, r, c, go)
                if event == trigger(leg, no):
                    when(lambda r, c: jnp.logical_not(condition(r, c)), r, c, go)

    begin(None)

    def put(side, i, k, value):
        high, low = split(value)
        side[0, i * BS : (i + 1) * BS, k * BS : (k + 1) * BS] = high
        side[1, i * BS : (i + 1) * BS, k * BS : (k + 1) * BS] = low

    def chosen(label, k, block):
        return jnp.where(label == float(k), block, 0.0)

    def assemble(side, forward, forward_labels, backward, backward_labels):
        for i in range(TAU):
            turned = backward(i).T
            for k in range(TAU):
                put(side, i, k, chosen(forward_labels(k), i, forward(k)) + chosen(backward_labels(i), k, turned))

    def multiply(s, left, right):
        for i in range(TAU):
            rows = slice(i * BS, (i + 1) * BS)
            high = left[0, rows, :]
            total = dot(high, right[1]) + dot(left[1, rows, :], right[0]) + dot(high, right[0])
            for j in range(TAU):
                out_ref[s, i, j] = total[:, j * BS : (j + 1) * BS]

    def form_onsite():
        labels = lambda t: jnp.full((1, BS), rows_ref[t, 0], jnp.int32).astype(jnp.float32)
        block = lambda t: onsite[t]
        side = sides.at[0, 0]
        assemble(side, block, labels, block, labels)
        multiply(0, side, side)

    def parts_of(src):
        place = pick(src, at, r, c)
        block = lambda t: buf[place, t, :BS, :]
        labels = lambda t: buf[place, t, BS : BS + 1, :]
        return block, labels

    arrived, formed = set(OWN), set()
    passing = max(number for number, leg in enumerate(legs) for later in legs if leg.name in names(later.src) | {later.after})
    for number, leg in enumerate(legs):
        when(leg.gets, r, c, copies[leg.name].wait_recv)
        arrived.add(leg.name)
        begin(leg.name)
        if number == 0:
            form_onsite()
        if number < passing:
            continue
        for s in range(1, STEPS):
            for at_side, pair in enumerate((final[s][:2], final[s][2:])):
                if (s, at_side) not in formed and arrived >= names(pair[0]) | names(pair[1]):
                    assemble(sides.at[s, at_side], *parts_of(pair[0]), *parts_of(pair[1]))
                    formed.add((s, at_side))
            if s not in formed and {(s, 0), (s, 1)} <= formed:
                multiply(s, sides.at[s, 0], sides.at[s, 1])
                formed.add(s)
    for leg in legs:
        when(leg.sends, r, c, copies[leg.name].wait_send)


def shards(u_blocks, u_rows):
    legs, final = plan()
    count = len(OWN) + len(legs)
    return pl.pallas_call(
        functools.partial(kernel, legs, final),
        out_shape=pltpu.VMEM((STEPS, TAU, TAU, BS, BS), jnp.float32),
        in_specs=[pl.BlockSpec(memory_space=pltpu.HBM)] * 2,
        out_specs=pl.BlockSpec(memory_space=pltpu.VMEM),
        scratch_shapes=[
            pltpu.VMEM((count, TAU, HEIGHT, BS), jnp.float32),
            pltpu.VMEM((TAU, BS, BS), jnp.float32),
            pltpu.SMEM((TAU, 2 * STEPS - 1), jnp.int32),
            pltpu.VMEM((STEPS, 2, 2, TAU * BS, TAU * BS), jnp.bfloat16),
            pltpu.SemaphoreType.DMA,
            pltpu.SemaphoreType.DMA((2 * STEPS - 1, TAU)),
            pltpu.SemaphoreType.DMA((len(legs),)),
            pltpu.SemaphoreType.DMA((len(legs),)),
        ],
        compiler_params=pltpu.CompilerParams(collective_id=0, has_side_effects=True, vmem_limit_bytes=40 << 20),
    )(*(pltpu.with_memory_space_constraint(each, pltpu.HBM) for each in (u_blocks, u_rows)))


def solution(mesh):
    return jax.shard_map(
        shards,
        mesh=mesh,
        in_specs=(P("row", "col", None, None), P("row", "col")),
        out_specs=P("row", "col", None, None, None),
        check_vma=False,
    )
```

```python
import functools

import jax
import jax.numpy as jnp
from jax import lax
from jax.experimental import pallas as pl
from jax.experimental.pallas import tpu as pltpu
from jax.sharding import PartitionSpec as P

MESH = pl.DeviceIdType.MESH
BS = 128
TAU = 3
STEPS = 4
N_ROW = 32
N_COL = 24
HEIGHT = BS + 8

RING = 8


def straight(k, m):
    return (
        lambda r, c: ((r + N_ROW - k) % N_ROW, (c + N_COL - m) % N_COL),
        lambda r, c: ((r + N_ROW + k) % N_ROW, (c + N_COL + m) % N_COL),
    )


def around(at, k):
    return at - at % RING + (at % RING + RING - k) % RING


def in_plane(k, m):
    return lambda r, c: (around(r, k), around(c, m)), lambda r, c: (around(r, -k), around(c, -m))


def in_row_plane(k, m):
    return (
        lambda r, c: (around(r, k), (c + N_COL - m) % N_COL),
        lambda r, c: (around(r, -k), (c + m) % N_COL),
    )


def wrapped(at, k):
    return jnp.where(at % RING >= RING - k, RING, 0)


def down(k, m):
    return (
        lambda r, c: ((r + N_ROW - wrapped(r, k)) % N_ROW, (c + N_COL - wrapped(c, m)) % N_COL),
        lambda r, c: ((r + wrapped(r, k)) % N_ROW, (c + wrapped(c, m)) % N_COL),
    )


class Leg:
    def __init__(self, name, src, move, sends=None):
        self.name, self.src, self.sends, self.after = name, src, sends, AFTER.get(name)
        self.to, self.origin = move
        self.gets = None if sends is None else lambda r, c: sends(*self.origin(r, c))


def plan():
    legs, final = {}, {}

    def leg(name, src, move, sends=None):
        legs[name] = Leg(name, src, move, sends)
        return name

    def late(name, src, k, m):
        crossed = lambda r, c: (r % RING >= RING - k) | (c % RING >= RING - m)
        leg(name, src, in_plane(k, m))
        leg(name + "z", name, down(k, m), crossed)
        return crossed, name + "z", name

    low = lambda k: lambda r, c: r % RING < k
    rows = lambda a, b: lambda r, c: (r % RING >= a) & (r % RING < b)
    wide = lambda r, c: c % RING >= 4

    leg("f3", "F3", straight(RING, 0), low(6))
    leg("fe3", (low(6), "f3", "F3"), in_plane(6, 0))
    leg("fm3", (low(3), "f3", "F3"), in_row_plane(3, 3))
    bs3 = leg("bs3", "B3", straight(0, 6))
    leg("bm3", bs3, straight(3, -3))
    final[3] = "fm3", bs3, "fe3", "bm3"

    leg("f2", "F2", straight(RING, 0), rows(2, 4))
    leg("fe2", (rows(2, 4), "f2", "F2"), in_plane(4, 0))
    leg("fe2z", "fe2", straight(RING, 0), rows(4, 6))
    leg("fm2", "F2", in_row_plane(2, 2), rows(2, 8))
    leg("fm2x", "fe2z", in_row_plane(-2, 2), rows(4, 6))
    leg("p2", "B2", in_plane(0, -2))
    leg("bs2", "p2", in_plane(0, -2))
    leg("bs2z", "bs2", down(0, 4), wide)
    bm2 = late("bm2", "B2", 2, 2)
    final[2] = (rows(6, 8), "fm2x", "fm2"), (wide, "bs2z", "bs2"), (rows(4, 6), "fe2z", "fe2"), bm2

    n1 = late("n1", "F1", 1, 0)
    c1 = leg("c1", "B1", straight(0, 1))
    fe1 = late("fe1", n1, 1, 0)
    fm1 = late("fm1", n1, 0, 1)
    leg("bm1", c1, straight(1, 0))
    leg("bs1", c1, straight(0, 1))
    final[1] = fm1, "bs1", fe1, "bm1"

    return [legs[name] for name in ORDER], final


ORDER = (
    "n1", "p2", "f3", "n1z", "fe1", "fm1", "f2", "fe2", "bs3", "fe2z", "bm2", "fe3", "c1", "fm1z", "bs2", "fe1z",
    "bm3", "bm1", "bm2z", "bs1", "fm2", "fm2x", "fm3", "bs2z",
)
AFTER = {"bm2": "n1", "bs2z": "fm1", "bs3": "n1", "c1": "f2", "fe2": "fm1", "fm3": "f2"}


OWN = ["F1", "F2", "F3", "B1", "B2", "B3"]


def places(legs):
    return {name: at for at, name in enumerate(OWN + [leg.name for leg in legs])}


def pick(src, at, r, c):
    if isinstance(src, str):
        return at[src]
    condition, yes, no = src
    return jnp.where(condition(r, c), at[yes], at[no])


def names(src):
    return {src} if isinstance(src, str) else set(src[1:])


def when(condition, r, c, do):
    if condition is None:
        do()
    else:
        pl.when(condition(r, c))(do)


def split(value):
    high = value.astype(jnp.bfloat16)
    return high, (value - high.astype(jnp.float32)).astype(jnp.bfloat16)


def dot(a, b):
    return jnp.dot(a, b, preferred_element_type=jnp.float32)


def kernel(legs, final, u_ref, rows_hbm, out_ref, buf, onsite, rows_ref, sides, rows_sem, load_sem, send_sem, recv_sem):
    r, c = lax.axis_index("row"), lax.axis_index("col")
    at = places(legs)
    copies = {}
    for number, leg in enumerate(legs):
        copies[leg.name] = pltpu.make_async_remote_copy(
            src_ref=buf.at[pick(leg.src, at, r, c)],
            dst_ref=buf.at[at[leg.name]],
            send_sem=send_sem.at[number],
            recv_sem=recv_sem.at[number],
            device_id=leg.to(r, c),
            device_id_type=MESH,
        )

    barrier = pltpu.get_barrier_semaphore()
    partners = 0
    for leg in legs:
        greet = functools.partial(
            pl.semaphore_signal, barrier, inc=1, device_id=leg.origin(r, c), device_id_type=MESH
        )
        when(leg.gets, r, c, greet)
        partners += 1 if leg.sends is None else jnp.where(leg.sends(r, c), 1, 0)

    loads = [pltpu.make_async_copy(rows_hbm, rows_ref, rows_sem)]
    loads[0].start()
    for j in range(2 * STEPS - 1):
        for t in range(TAU):
            target = onsite.at[t] if j == 0 else buf.at[j - 1, t, pl.ds(0, BS)]
            loads.append(pltpu.make_async_copy(u_ref.at[t, j], target, load_sem.at[j, t]))
            loads[-1].start()
    loads[0].wait()
    for j in range(1, 2 * STEPS - 1):
        for t in range(TAU):
            buf[j - 1, t, BS:HEIGHT, :] = jnp.full((HEIGHT - BS, BS), rows_ref[t, j], jnp.int32).astype(jnp.float32)
    for load in loads[1:]:
        load.wait()
    pl.semaphore_wait(barrier, partners)

    rank = {None: -1, **{leg.name: number for number, leg in enumerate(legs)}}

    def trigger(leg, source):
        return max(None if source in OWN else source, leg.after, key=rank.get)

    def begin(event):
        for leg in legs:
            go = copies[leg.name].start
            if isinstance(leg.src, str):
                if event == trigger(leg, leg.src):
                    when(leg.sends, r, c, go)
            else:
                condition, yes, no = leg.src
                if event == trigger(leg, yes):
                    when(condition, r, c, go)
                if event == trigger(leg, no):
                    when(lambda r, c: jnp.logical_not(condition(r, c)), r, c, go)

    begin(None)

    def put(side, i, k, value):
        high, low = split(value)
        side[0, i * BS : (i + 1) * BS, k * BS : (k + 1) * BS] = high
        side[1, i * BS : (i + 1) * BS, k * BS : (k + 1) * BS] = low

    def chosen(label, k, block):
        return jnp.where(label == float(k), block, 0.0)

    def assemble(side, forward, forward_labels, backward, backward_labels):
        for i in range(TAU):
            turned = backward(i).T
            for k in range(TAU):
                put(side, i, k, chosen(forward_labels(k), i, forward(k)) + chosen(backward_labels(i), k, turned))

    def multiply(s, left, right):
        for i in range(TAU):
            rows = slice(i * BS, (i + 1) * BS)
            high = left[0, rows, :]
            total = dot(high, right[1]) + dot(left[1, rows, :], right[0]) + dot(high, right[0])
            for j in range(TAU):
                out_ref[s, i, j] = total[:, j * BS : (j + 1) * BS]

    def form_onsite():
        labels = lambda t: jnp.full((1, BS), rows_ref[t, 0], jnp.int32).astype(jnp.float32)
        block = lambda t: onsite[t]
        side = sides.at[0, 0]
        assemble(side, block, labels, block, labels)
        multiply(0, side, side)

    def parts_of(src):
        place = pick(src, at, r, c)
        block = lambda t: buf[place, t, :BS, :]
        labels = lambda t: buf[place, t, BS : BS + 1, :]
        return block, labels

    arrived, formed = set(OWN), set()
    passing = max(number for number, leg in enumerate(legs) for later in legs if leg.name in names(later.src) | {later.after})
    for number, leg in enumerate(legs):
        when(leg.gets, r, c, copies[leg.name].wait_recv)
        arrived.add(leg.name)
        begin(leg.name)
        if number == 0:
            form_onsite()
        if number < passing:
            continue
        for s in range(1, STEPS):
            for at_side, pair in enumerate((final[s][:2], final[s][2:])):
                if (s, at_side) not in formed and arrived >= names(pair[0]) | names(pair[1]):
                    assemble(sides.at[s, at_side], *parts_of(pair[0]), *parts_of(pair[1]))
                    formed.add((s, at_side))
            if s not in formed and {(s, 0), (s, 1)} <= formed:
                multiply(s, sides.at[s, 0], sides.at[s, 1])
                formed.add(s)
    for leg in legs:
        when(leg.sends, r, c, copies[leg.name].wait_send)


def shards(u_blocks, u_rows):
    legs, final = plan()
    count = len(OWN) + len(legs)
    return pl.pallas_call(
        functools.partial(kernel, legs, final),
        out_shape=pltpu.VMEM((STEPS, TAU, TAU, BS, BS), jnp.float32),
        in_specs=[pl.BlockSpec(memory_space=pltpu.HBM)] * 2,
        out_specs=pl.BlockSpec(memory_space=pltpu.VMEM),
        scratch_shapes=[
            pltpu.VMEM((count, TAU, HEIGHT, BS), jnp.float32),
            pltpu.VMEM((TAU, BS, BS), jnp.float32),
            pltpu.SMEM((TAU, 2 * STEPS - 1), jnp.int32),
            pltpu.VMEM((STEPS, 2, 2, TAU * BS, TAU * BS), jnp.bfloat16),
            pltpu.SemaphoreType.DMA,
            pltpu.SemaphoreType.DMA((2 * STEPS - 1, TAU)),
            pltpu.SemaphoreType.DMA((len(legs),)),
            pltpu.SemaphoreType.DMA((len(legs),)),
        ],
        compiler_params=pltpu.CompilerParams(collective_id=0, has_side_effects=True, vmem_limit_bytes=40 << 20),
    )(*(pltpu.with_memory_space_constraint(each, pltpu.HBM) for each in (u_blocks, u_rows)))


def solution(mesh):
    return jax.shard_map(
        shards,
        mesh=mesh,
        in_specs=(P("row", "col", None, None), P("row", "col")),
        out_specs=P("row", "col", None, None, None),
        check_vma=False,
    )
```

```python
import functools

import jax
import jax.numpy as jnp
from jax import lax
from jax.experimental import pallas as pl
from jax.experimental.pallas import tpu as pltpu
from jax.sharding import PartitionSpec as P

MESH = pl.DeviceIdType.MESH
BS = 128
TAU = 3
STEPS = 4
N_ROW = 32
N_COL = 24
HEIGHT = BS + 8

RING = 8


def straight(k, m):
    return (
        lambda r, c: ((r + N_ROW - k) % N_ROW, (c + N_COL - m) % N_COL),
        lambda r, c: ((r + N_ROW + k) % N_ROW, (c + N_COL + m) % N_COL),
    )


def around(at, k):
    return at - at % RING + (at % RING + RING - k) % RING


def in_plane(k, m):
    return lambda r, c: (around(r, k), around(c, m)), lambda r, c: (around(r, -k), around(c, -m))


def in_row_plane(k, m):
    return (
        lambda r, c: (around(r, k), (c + N_COL - m) % N_COL),
        lambda r, c: (around(r, -k), (c + m) % N_COL),
    )


def wrapped(at, k):
    return jnp.where(at % RING >= RING - k, RING, 0)


def down(k, m):
    return (
        lambda r, c: ((r + N_ROW - wrapped(r, k)) % N_ROW, (c + N_COL - wrapped(c, m)) % N_COL),
        lambda r, c: ((r + wrapped(r, k)) % N_ROW, (c + wrapped(c, m)) % N_COL),
    )


class Leg:
    def __init__(self, name, src, move, sends=None):
        self.name, self.src, self.sends, self.after = name, src, sends, AFTER.get(name)
        self.to, self.origin = move
        self.gets = None if sends is None else lambda r, c: sends(*self.origin(r, c))


def plan():
    legs, final = {}, {}

    def leg(name, src, move, sends=None):
        legs[name] = Leg(name, src, move, sends)
        return name

    def late(name, src, k, m):
        crossed = lambda r, c: (r % RING >= RING - k) | (c % RING >= RING - m)
        leg(name, src, in_plane(k, m))
        leg(name + "z", name, down(k, m), crossed)
        return crossed, name + "z", name

    low = lambda k: lambda r, c: r % RING < k
    rows = lambda a, b: lambda r, c: (r % RING >= a) & (r % RING < b)
    wide = lambda r, c: c % RING >= 4

    leg("f3", "F3", straight(RING, 0), low(6))
    leg("fe3", (low(6), "f3", "F3"), in_plane(6, 0))
    leg("fm3", (low(3), "f3", "F3"), in_row_plane(3, 3))
    bs3 = leg("bs3", "B3", straight(0, 6))
    leg("bm3", bs3, straight(3, -3))
    final[3] = "fm3", bs3, "fe3", "bm3"

    leg("f2", "F2", straight(RING, 0), rows(2, 4))
    leg("fe2", (rows(2, 4), "f2", "F2"), in_plane(4, 0))
    leg("fe2z", "fe2", straight(RING, 0), rows(4, 6))
    leg("n2", "F2", in_plane(2, 0), rows(2, 6))
    leg("fm2a", "n2", straight(0, 2), rows(0, 4))
    leg("fm2", "F2", in_row_plane(2, 2), rows(6, 8))
    leg("fm2x", "fe2z", in_row_plane(-2, 2), rows(4, 6))
    leg("p2", "B2", in_plane(0, -2))
    leg("bs2", "p2", in_plane(0, -2))
    leg("bs2z", "bs2", down(0, 4), wide)
    bm2 = late("bm2", "B2", 2, 2)
    final[2] = (rows(6, 8), "fm2x", (rows(0, 4), "fm2a", "fm2")), (wide, "bs2z", "bs2"), (rows(4, 6), "fe2z", "fe2"), bm2

    n1 = late("n1", "F1", 1, 0)
    c1 = leg("c1", "B1", straight(0, 1))
    fe1 = late("fe1", n1, 1, 0)
    fm1 = late("fm1", n1, 0, 1)
    leg("bm1", c1, straight(1, 0))
    leg("bs1", c1, straight(0, 1))
    final[1] = fm1, "bs1", fe1, "bm1"

    return [legs[name] for name in ORDER], final


ORDER = (
    "n1", "n1z", "n2", "p2", "fe1", "fm1", "bm2", "f2", "bs3", "f3", "fe2", "c1", "fe2z", "fe3", "bs2", "bm3",
    "bm1", "fm1z", "bs1", "fe1z", "bm2z", "fm3", "bs2z", "fm2", "fm2a", "fm2x",
)
AFTER = {"bm1": "fm1", "bm2": "n1", "bm3": "fm1", "bs1": "fm1", "bs2": "fm1", "bs3": "n1", "f3": "n1", "fe2": "fe1", "fe3": "fm1", "fm3": "f2"}


OWN = ["F1", "F2", "F3", "B1", "B2", "B3"]


def places(legs):
    return {name: at for at, name in enumerate(OWN + [leg.name for leg in legs])}


def pick(src, at, r, c):
    if isinstance(src, str):
        return at[src]
    condition, yes, no = src
    return jnp.where(condition(r, c), pick(yes, at, r, c), pick(no, at, r, c))


def names(src):
    return {src} if isinstance(src, str) else names(src[1]) | names(src[2])


def when(condition, r, c, do):
    if condition is None:
        do()
    else:
        pl.when(condition(r, c))(do)


def split(value):
    high = value.astype(jnp.bfloat16)
    return high, (value - high.astype(jnp.float32)).astype(jnp.bfloat16)


def dot(a, b):
    return jnp.dot(a, b, preferred_element_type=jnp.float32)


def kernel(legs, final, u_ref, rows_hbm, out_ref, buf, onsite, rows_ref, sides, rows_sem, load_sem, send_sem, recv_sem):
    r, c = lax.axis_index("row"), lax.axis_index("col")
    at = places(legs)
    copies = {}
    for number, leg in enumerate(legs):
        copies[leg.name] = pltpu.make_async_remote_copy(
            src_ref=buf.at[pick(leg.src, at, r, c)],
            dst_ref=buf.at[at[leg.name]],
            send_sem=send_sem.at[number],
            recv_sem=recv_sem.at[number],
            device_id=leg.to(r, c),
            device_id_type=MESH,
        )

    barrier = pltpu.get_barrier_semaphore()
    partners = 0
    for leg in legs:
        greet = functools.partial(
            pl.semaphore_signal, barrier, inc=1, device_id=leg.origin(r, c), device_id_type=MESH
        )
        when(leg.gets, r, c, greet)
        partners += 1 if leg.sends is None else jnp.where(leg.sends(r, c), 1, 0)

    loads = [pltpu.make_async_copy(rows_hbm, rows_ref, rows_sem)]
    loads[0].start()
    for j in range(2 * STEPS - 1):
        for t in range(TAU):
            target = onsite.at[t] if j == 0 else buf.at[j - 1, t, pl.ds(0, BS)]
            loads.append(pltpu.make_async_copy(u_ref.at[t, j], target, load_sem.at[j, t]))
            loads[-1].start()
    loads[0].wait()
    for j in range(1, 2 * STEPS - 1):
        for t in range(TAU):
            buf[j - 1, t, BS:HEIGHT, :] = jnp.full((HEIGHT - BS, BS), rows_ref[t, j], jnp.int32).astype(jnp.float32)
    for load in loads[1:]:
        load.wait()
    pl.semaphore_wait(barrier, partners)

    rank = {None: -1, **{leg.name: number for number, leg in enumerate(legs)}}

    def trigger(leg, source):
        return max(None if source in OWN else source, leg.after, key=rank.get)

    def begin(event):
        for leg in legs:
            go = copies[leg.name].start
            if isinstance(leg.src, str):
                if event == trigger(leg, leg.src):
                    when(leg.sends, r, c, go)
            else:
                condition, yes, no = leg.src
                if event == trigger(leg, yes):
                    when(condition, r, c, go)
                if event == trigger(leg, no):
                    when(lambda r, c: jnp.logical_not(condition(r, c)), r, c, go)

    begin(None)

    def put(side, i, k, value):
        high, low = split(value)
        side[0, i * BS : (i + 1) * BS, k * BS : (k + 1) * BS] = high
        side[1, i * BS : (i + 1) * BS, k * BS : (k + 1) * BS] = low

    def chosen(label, k, block):
        return jnp.where(label == float(k), block, 0.0)

    def assemble(side, forward, forward_labels, backward, backward_labels):
        for i in range(TAU):
            turned = backward(i).T
            for k in range(TAU):
                put(side, i, k, chosen(forward_labels(k), i, forward(k)) + chosen(backward_labels(i), k, turned))

    def multiply(s, left, right):
        for i in range(TAU):
            rows = slice(i * BS, (i + 1) * BS)
            high = left[0, rows, :]
            total = dot(high, right[1]) + dot(left[1, rows, :], right[0]) + dot(high, right[0])
            for j in range(TAU):
                out_ref[s, i, j] = total[:, j * BS : (j + 1) * BS]

    def form_onsite():
        labels = lambda t: jnp.full((1, BS), rows_ref[t, 0], jnp.int32).astype(jnp.float32)
        block = lambda t: onsite[t]
        side = sides.at[0, 0]
        assemble(side, block, labels, block, labels)
        multiply(0, side, side)

    def parts_of(src):
        place = pick(src, at, r, c)
        block = lambda t: buf[place, t, :BS, :]
        labels = lambda t: buf[place, t, BS : BS + 1, :]
        return block, labels

    arrived, formed = set(OWN), set()
    passing = max(number for number, leg in enumerate(legs) for later in legs if leg.name in names(later.src) | {later.after})
    for number, leg in enumerate(legs):
        when(leg.gets, r, c, copies[leg.name].wait_recv)
        arrived.add(leg.name)
        begin(leg.name)
        if number == 0:
            form_onsite()
        if number < passing:
            continue
        for s in range(1, STEPS):
            for at_side, pair in enumerate((final[s][:2], final[s][2:])):
                if (s, at_side) not in formed and arrived >= names(pair[0]) | names(pair[1]):
                    assemble(sides.at[s, at_side], *parts_of(pair[0]), *parts_of(pair[1]))
                    formed.add((s, at_side))
            if s not in formed and {(s, 0), (s, 1)} <= formed:
                multiply(s, sides.at[s, 0], sides.at[s, 1])
                formed.add(s)
    for leg in legs:
        when(leg.sends, r, c, copies[leg.name].wait_send)


def shards(u_blocks, u_rows):
    legs, final = plan()
    count = len(OWN) + len(legs)
    return pl.pallas_call(
        functools.partial(kernel, legs, final),
        out_shape=pltpu.VMEM((STEPS, TAU, TAU, BS, BS), jnp.float32),
        in_specs=[pl.BlockSpec(memory_space=pltpu.HBM)] * 2,
        out_specs=pl.BlockSpec(memory_space=pltpu.VMEM),
        scratch_shapes=[
            pltpu.VMEM((count, TAU, HEIGHT, BS), jnp.float32),
            pltpu.VMEM((TAU, BS, BS), jnp.float32),
            pltpu.SMEM((TAU, 2 * STEPS - 1), jnp.int32),
            pltpu.VMEM((STEPS, 2, 2, TAU * BS, TAU * BS), jnp.bfloat16),
            pltpu.SemaphoreType.DMA,
            pltpu.SemaphoreType.DMA((2 * STEPS - 1, TAU)),
            pltpu.SemaphoreType.DMA((len(legs),)),
            pltpu.SemaphoreType.DMA((len(legs),)),
        ],
        compiler_params=pltpu.CompilerParams(collective_id=0, has_side_effects=True, vmem_limit_bytes=40 << 20),
    )(*(pltpu.with_memory_space_constraint(each, pltpu.HBM) for each in (u_blocks, u_rows)))


def solution(mesh):
    return jax.shard_map(
        shards,
        mesh=mesh,
        in_specs=(P("row", "col", None, None), P("row", "col")),
        out_specs=P("row", "col", None, None, None),
        check_vma=False,
    )
```

```python
import functools

import jax
import jax.numpy as jnp
from jax import lax
from jax.experimental import pallas as pl
from jax.experimental.pallas import tpu as pltpu
from jax.sharding import PartitionSpec as P

MESH = pl.DeviceIdType.MESH
BS = 128
TAU = 3
STEPS = 4
N_ROW = 32
N_COL = 24
HEIGHT = BS + 8

RING = 8


def straight(k, m):
    return (
        lambda r, c: ((r + N_ROW - k) % N_ROW, (c + N_COL - m) % N_COL),
        lambda r, c: ((r + N_ROW + k) % N_ROW, (c + N_COL + m) % N_COL),
    )


def around(at, k):
    return at - at % RING + (at % RING + RING - k) % RING


def in_plane(k, m):
    return lambda r, c: (around(r, k), around(c, m)), lambda r, c: (around(r, -k), around(c, -m))


def in_row_plane(k, m):
    return (
        lambda r, c: (around(r, k), (c + N_COL - m) % N_COL),
        lambda r, c: (around(r, -k), (c + m) % N_COL),
    )


def wrapped(at, k):
    return jnp.where(at % RING >= RING - k, RING, 0)


def down(k, m):
    return (
        lambda r, c: ((r + N_ROW - wrapped(r, k)) % N_ROW, (c + N_COL - wrapped(c, m)) % N_COL),
        lambda r, c: ((r + wrapped(r, k)) % N_ROW, (c + wrapped(c, m)) % N_COL),
    )


class Leg:
    def __init__(self, name, src, move, sends=None):
        self.name, self.src, self.sends, self.after = name, src, sends, AFTER.get(name)
        self.to, self.origin = move
        self.gets = None if sends is None else lambda r, c: sends(*self.origin(r, c))


def plan():
    legs, final = {}, {}

    def leg(name, src, move, sends=None):
        legs[name] = Leg(name, src, move, sends)
        return name

    def late(name, src, k, m):
        crossed = lambda r, c: (r % RING >= RING - k) | (c % RING >= RING - m)
        leg(name, src, in_plane(k, m))
        leg(name + "z", name, down(k, m), crossed)
        return crossed, name + "z", name

    low = lambda k: lambda r, c: r % RING < k
    rows = lambda a, b: lambda r, c: (r % RING >= a) & (r % RING < b)
    wide = lambda r, c: c % RING >= 4

    leg("f3", "F3", straight(RING, 0), low(6))
    leg("fe3", (low(6), "f3", "F3"), in_plane(6, 0))
    leg("fm3", (low(3), "f3", "F3"), in_row_plane(3, 3))
    bs3 = late("bs3", "B3", 0, 6)
    leg("bm3", bs3, straight(3, -3))
    final[3] = "fm3", bs3, "fe3", "bm3"

    leg("f2", "F2", straight(RING, 0), rows(2, 4))
    leg("fe2", (rows(2, 4), "f2", "F2"), in_plane(4, 0))
    leg("fe2z", "fe2", straight(RING, 0), rows(4, 6))
    leg("fm2", "F2", in_row_plane(2, 2), rows(2, 8))
    leg("fm2x", "fe2z", in_row_plane(-2, 2), rows(4, 6))
    leg("p2", "B2", in_plane(0, -2))
    leg("bs2", "p2", in_plane(0, -2))
    leg("bs2z", "bs2", down(0, 4), wide)
    bm2 = late("bm2", "B2", 2, 2)
    final[2] = (rows(6, 8), "fm2x", "fm2"), (wide, "bs2z", "bs2"), (rows(4, 6), "fe2z", "fe2"), bm2

    n1 = late("n1", "F1", 1, 0)
    c1 = leg("c1", "B1", straight(0, 1))
    fe1 = late("fe1", n1, 1, 0)
    fm1 = late("fm1", n1, 0, 1)
    leg("bm1", c1, straight(1, 0))
    leg("bs1", c1, straight(0, 1))
    final[1] = fm1, "bs1", fe1, "bm1"

    return [legs[name] for name in ORDER], final


ORDER = (
    "n1", "n1z", "p2", "fe1", "fe1z", "f3", "f2", "bs3", "fm1", "bs3z", "fe2", "fe2z", "bm2", "c1", "bs2", "fe3",
    "bm1", "fm3", "bs1", "fm2", "fm2x", "bm3", "fm1z", "bm2z", "bs2z",
)
AFTER = {"bm2": "n1", "c1": "bs3", "f2": "n1", "f3": "n1", "fe2": "n1", "fm3": "f2", "p2": "n1"}


OWN = ["F1", "F2", "F3", "B1", "B2", "B3"]


def places(legs):
    return {name: at for at, name in enumerate(OWN + [leg.name for leg in legs])}


def pick(src, at, r, c):
    if isinstance(src, str):
        return at[src]
    condition, yes, no = src
    return jnp.where(condition(r, c), at[yes], at[no])


def names(src):
    return {src} if isinstance(src, str) else set(src[1:])


def when(condition, r, c, do):
    if condition is None:
        do()
    else:
        pl.when(condition(r, c))(do)


def split(value):
    high = value.astype(jnp.bfloat16)
    return high, (value - high.astype(jnp.float32)).astype(jnp.bfloat16)


def dot(a, b):
    return jnp.dot(a, b, preferred_element_type=jnp.float32)


def kernel(legs, final, u_ref, rows_hbm, out_ref, buf, onsite, rows_ref, sides, rows_sem, load_sem, send_sem, recv_sem):
    r, c = lax.axis_index("row"), lax.axis_index("col")
    at = places(legs)
    copies = {}
    for number, leg in enumerate(legs):
        copies[leg.name] = pltpu.make_async_remote_copy(
            src_ref=buf.at[pick(leg.src, at, r, c)],
            dst_ref=buf.at[at[leg.name]],
            send_sem=send_sem.at[number],
            recv_sem=recv_sem.at[number],
            device_id=leg.to(r, c),
            device_id_type=MESH,
        )

    barrier = pltpu.get_barrier_semaphore()
    partners = 0
    for leg in legs:
        greet = functools.partial(
            pl.semaphore_signal, barrier, inc=1, device_id=leg.origin(r, c), device_id_type=MESH
        )
        when(leg.gets, r, c, greet)
        partners += 1 if leg.sends is None else jnp.where(leg.sends(r, c), 1, 0)

    loads = [pltpu.make_async_copy(rows_hbm, rows_ref, rows_sem)]
    loads[0].start()
    for j in range(2 * STEPS - 1):
        for t in range(TAU):
            target = onsite.at[t] if j == 0 else buf.at[j - 1, t, pl.ds(0, BS)]
            loads.append(pltpu.make_async_copy(u_ref.at[t, j], target, load_sem.at[j, t]))
            loads[-1].start()
    loads[0].wait()
    for j in range(1, 2 * STEPS - 1):
        for t in range(TAU):
            buf[j - 1, t, BS:HEIGHT, :] = jnp.full((HEIGHT - BS, BS), rows_ref[t, j], jnp.int32).astype(jnp.float32)
    for load in loads[1:]:
        load.wait()
    pl.semaphore_wait(barrier, partners)

    rank = {None: -1, **{leg.name: number for number, leg in enumerate(legs)}}

    def trigger(leg, source):
        return max(None if source in OWN else source, leg.after, key=rank.get)

    def begin(event):
        for leg in legs:
            go = copies[leg.name].start
            if isinstance(leg.src, str):
                if event == trigger(leg, leg.src):
                    when(leg.sends, r, c, go)
            else:
                condition, yes, no = leg.src
                if event == trigger(leg, yes):
                    when(condition, r, c, go)
                if event == trigger(leg, no):
                    when(lambda r, c: jnp.logical_not(condition(r, c)), r, c, go)

    begin(None)

    def put(side, i, k, value):
        high, low = split(value)
        side[0, i * BS : (i + 1) * BS, k * BS : (k + 1) * BS] = high
        side[1, i * BS : (i + 1) * BS, k * BS : (k + 1) * BS] = low

    def chosen(label, k, block):
        return jnp.where(label == float(k), block, 0.0)

    def assemble(side, forward, forward_labels, backward, backward_labels):
        for i in range(TAU):
            turned = backward(i).T
            for k in range(TAU):
                put(side, i, k, chosen(forward_labels(k), i, forward(k)) + chosen(backward_labels(i), k, turned))

    def multiply(s, left, right):
        for i in range(TAU):
            rows = slice(i * BS, (i + 1) * BS)
            high = left[0, rows, :]
            total = dot(high, right[1]) + dot(left[1, rows, :], right[0]) + dot(high, right[0])
            for j in range(TAU):
                out_ref[s, i, j] = total[:, j * BS : (j + 1) * BS]

    def form_onsite():
        labels = lambda t: jnp.full((1, BS), rows_ref[t, 0], jnp.int32).astype(jnp.float32)
        block = lambda t: onsite[t]
        side = sides.at[0, 0]
        assemble(side, block, labels, block, labels)
        multiply(0, side, side)

    def parts_of(src):
        place = pick(src, at, r, c)
        block = lambda t: buf[place, t, :BS, :]
        labels = lambda t: buf[place, t, BS : BS + 1, :]
        return block, labels

    arrived, formed = set(OWN), set()
    passing = max(number for number, leg in enumerate(legs) for later in legs if leg.name in names(later.src) | {later.after})
    for number, leg in enumerate(legs):
        when(leg.gets, r, c, copies[leg.name].wait_recv)
        arrived.add(leg.name)
        begin(leg.name)
        if number == 0:
            form_onsite()
        if number < passing:
            continue
        for s in range(1, STEPS):
            for at_side, pair in enumerate((final[s][:2], final[s][2:])):
                if (s, at_side) not in formed and arrived >= names(pair[0]) | names(pair[1]):
                    assemble(sides.at[s, at_side], *parts_of(pair[0]), *parts_of(pair[1]))
                    formed.add((s, at_side))
            if s not in formed and {(s, 0), (s, 1)} <= formed:
                multiply(s, sides.at[s, 0], sides.at[s, 1])
                formed.add(s)
    for leg in legs:
        when(leg.sends, r, c, copies[leg.name].wait_send)


def shards(u_blocks, u_rows):
    legs, final = plan()
    count = len(OWN) + len(legs)
    return pl.pallas_call(
        functools.partial(kernel, legs, final),
        out_shape=pltpu.VMEM((STEPS, TAU, TAU, BS, BS), jnp.float32),
        in_specs=[pl.BlockSpec(memory_space=pltpu.HBM)] * 2,
        out_specs=pl.BlockSpec(memory_space=pltpu.VMEM),
        scratch_shapes=[
            pltpu.VMEM((count, TAU, HEIGHT, BS), jnp.float32),
            pltpu.VMEM((TAU, BS, BS), jnp.float32),
            pltpu.SMEM((TAU, 2 * STEPS - 1), jnp.int32),
            pltpu.VMEM((STEPS, 2, 2, TAU * BS, TAU * BS), jnp.bfloat16),
            pltpu.SemaphoreType.DMA,
            pltpu.SemaphoreType.DMA((2 * STEPS - 1, TAU)),
            pltpu.SemaphoreType.DMA((len(legs),)),
            pltpu.SemaphoreType.DMA((len(legs),)),
        ],
        compiler_params=pltpu.CompilerParams(collective_id=0, has_side_effects=True, vmem_limit_bytes=40 << 20),
    )(*(pltpu.with_memory_space_constraint(each, pltpu.HBM) for each in (u_blocks, u_rows)))


def solution(mesh):
    return jax.shard_map(
        shards,
        mesh=mesh,
        in_specs=(P("row", "col", None, None), P("row", "col")),
        out_specs=P("row", "col", None, None, None),
        check_vma=False,
    )
```

```python
import functools

import jax
import jax.numpy as jnp
from jax import lax
from jax.experimental import pallas as pl
from jax.experimental.pallas import tpu as pltpu
from jax.sharding import PartitionSpec as P

MESH = pl.DeviceIdType.MESH
BS = 128
TAU = 3
STEPS = 4
N_ROW = 32
N_COL = 24
HEIGHT = BS + 8

RING = 8


def straight(k, m):
    return (
        lambda r, c: ((r + N_ROW - k) % N_ROW, (c + N_COL - m) % N_COL),
        lambda r, c: ((r + N_ROW + k) % N_ROW, (c + N_COL + m) % N_COL),
    )


def around(at, k):
    return at - at % RING + (at % RING + RING - k) % RING


def in_plane(k, m):
    return lambda r, c: (around(r, k), around(c, m)), lambda r, c: (around(r, -k), around(c, -m))


def in_row_plane(k, m):
    return (
        lambda r, c: (around(r, k), (c + N_COL - m) % N_COL),
        lambda r, c: (around(r, -k), (c + m) % N_COL),
    )


def wrapped(at, k):
    return jnp.where(at % RING >= RING - k, RING, 0)


def down(k, m):
    return (
        lambda r, c: ((r + N_ROW - wrapped(r, k)) % N_ROW, (c + N_COL - wrapped(c, m)) % N_COL),
        lambda r, c: ((r + wrapped(r, k)) % N_ROW, (c + wrapped(c, m)) % N_COL),
    )


class Leg:
    def __init__(self, name, src, move, sends=None):
        self.name, self.src, self.sends, self.after = name, src, sends, AFTER.get(name)
        self.to, self.origin = move
        self.gets = None if sends is None else lambda r, c: sends(*self.origin(r, c))


def plan():
    legs, final = {}, {}

    def leg(name, src, move, sends=None):
        legs[name] = Leg(name, src, move, sends)
        return name

    def late(name, src, k, m):
        crossed = lambda r, c: (r % RING >= RING - k) | (c % RING >= RING - m)
        leg(name, src, in_plane(k, m))
        leg(name + "z", name, down(k, m), crossed)
        return crossed, name + "z", name

    low = lambda k: lambda r, c: r % RING < k
    rows = lambda a, b: lambda r, c: (r % RING >= a) & (r % RING < b)
    wide = lambda r, c: c % RING >= 4

    leg("f3", "F3", straight(RING, 0), low(6))
    leg("fe3", (low(6), "f3", "F3"), in_plane(6, 0))
    leg("fm3", (low(3), "f3", "F3"), in_row_plane(3, 3))
    bs3 = late("bs3", "B3", 0, 6)
    leg("bm3", bs3, straight(3, -3))
    final[3] = "fm3", bs3, "fe3", "bm3"

    leg("f2", "F2", straight(RING, 0), rows(2, 4))
    leg("fe2", (rows(2, 4), "f2", "F2"), in_plane(4, 0))
    leg("fe2z", "fe2", straight(RING, 0), rows(4, 6))
    leg("fm2", "F2", in_row_plane(2, 2), rows(2, 8))
    leg("fm2x", "fe2z", in_row_plane(-2, 2), rows(4, 6))
    leg("p2", "B2", in_plane(0, -2))
    leg("bs2", "p2", in_plane(0, -2))
    leg("bs2z", "bs2", down(0, 4), wide)
    bm2 = late("bm2", "B2", 2, 2)
    final[2] = (rows(6, 8), "fm2x", "fm2"), (wide, "bs2z", "bs2"), (rows(4, 6), "fe2z", "fe2"), bm2

    n1 = late("n1", "F1", 1, 0)
    c1 = leg("c1", "B1", straight(0, 1))
    fe1 = late("fe1", n1, 1, 0)
    fm1 = late("fm1", n1, 0, 1)
    leg("bm1", c1, straight(1, 0))
    leg("bs1", c1, straight(0, 1))
    final[1] = fm1, "bs1", fe1, "bm1"

    return [legs[name] for name in ORDER], final


ORDER = (
    "n1", "n1z", "p2", "fe1", "fe1z", "f3", "f2", "bs3", "fm1", "bs3z", "fe2", "fe2z", "bm2", "c1", "bs2", "fe3",
    "bm1", "fm3", "bs1", "fm2", "fm2x", "bm3", "fm1z", "bm2z", "bs2z",
)
AFTER = {"bm2": "n1", "c1": "bs3", "f2": "n1", "f3": "n1", "fe2": "n1", "fm3": "f2", "p2": "n1"}


OWN = ["F1", "F2", "F3", "B1", "B2", "B3"]


def places(legs):
    return {name: at for at, name in enumerate(OWN + [leg.name for leg in legs])}


def pick(src, at, r, c):
    if isinstance(src, str):
        return at[src]
    condition, yes, no = src
    return jnp.where(condition(r, c), at[yes], at[no])


def names(src):
    return {src} if isinstance(src, str) else set(src[1:])


def when(condition, r, c, do):
    if condition is None:
        do()
    else:
        pl.when(condition(r, c))(do)


def split(value):
    high = value.astype(jnp.bfloat16)
    return high, (value - high.astype(jnp.float32)).astype(jnp.bfloat16)


def dot(a, b):
    return jnp.dot(a, b, preferred_element_type=jnp.float32)


def kernel(legs, final, u_ref, rows_hbm, out_ref, buf, onsite, rows_ref, sides, rows_sem, load_sem, send_sem, recv_sem):
    r, c = lax.axis_index("row"), lax.axis_index("col")
    at = places(legs)
    copies = {}
    for number, leg in enumerate(legs):
        copies[leg.name] = pltpu.make_async_remote_copy(
            src_ref=buf.at[pick(leg.src, at, r, c)],
            dst_ref=buf.at[at[leg.name]],
            send_sem=send_sem.at[number],
            recv_sem=recv_sem.at[number],
            device_id=leg.to(r, c),
            device_id_type=MESH,
        )

    barrier = pltpu.get_barrier_semaphore()
    partners = 0
    for leg in legs:
        greet = functools.partial(
            pl.semaphore_signal, barrier, inc=1, device_id=leg.origin(r, c), device_id_type=MESH
        )
        when(leg.gets, r, c, greet)
        partners += 1 if leg.sends is None else jnp.where(leg.sends(r, c), 1, 0)

    labels_load = pltpu.make_async_copy(rows_hbm, rows_ref, rows_sem)
    labels_load.start()
    loads = {}
    for j in (1, 6, 2, 3, 5, 4, 0):
        loads[j] = []
        for t in range(TAU):
            target = onsite.at[t] if j == 0 else buf.at[j - 1, t, pl.ds(0, BS)]
            loads[j].append(pltpu.make_async_copy(u_ref.at[t, j], target, load_sem.at[j, t]))
            loads[j][-1].start()
    labels_load.wait()
    for j in range(1, 2 * STEPS - 1):
        for t in range(TAU):
            buf[j - 1, t, BS:HEIGHT, :] = jnp.full((HEIGHT - BS, BS), rows_ref[t, j], jnp.int32).astype(jnp.float32)
    pl.semaphore_wait(barrier, partners)

    def loaded(j):
        for load in loads.pop(j, ()):
            load.wait()

    rank = {None: -1, **{leg.name: number for number, leg in enumerate(legs)}}

    def trigger(leg, source):
        return max(None if source in OWN else source, leg.after, key=rank.get)

    def begin(event):
        for leg in legs:
            go = copies[leg.name].start
            if event is None:
                own = leg.src if isinstance(leg.src, str) else leg.src[2]
                if own in OWN and trigger(leg, own) is None:
                    loaded(1 + OWN.index(own))
            if isinstance(leg.src, str):
                if event == trigger(leg, leg.src):
                    when(leg.sends, r, c, go)
            else:
                condition, yes, no = leg.src
                if event == trigger(leg, yes):
                    when(condition, r, c, go)
                if event == trigger(leg, no):
                    when(lambda r, c: jnp.logical_not(condition(r, c)), r, c, go)

    begin(None)
    for j in list(loads):
        loaded(j)

    def put(side, i, k, value):
        high, low = split(value)
        side[0, i * BS : (i + 1) * BS, k * BS : (k + 1) * BS] = high
        side[1, i * BS : (i + 1) * BS, k * BS : (k + 1) * BS] = low

    def chosen(label, k, block):
        return jnp.where(label == float(k), block, 0.0)

    def assemble(side, forward, forward_labels, backward, backward_labels):
        for i in range(TAU):
            turned = backward(i).T
            for k in range(TAU):
                put(side, i, k, chosen(forward_labels(k), i, forward(k)) + chosen(backward_labels(i), k, turned))

    def multiply(s, left, right):
        for i in range(TAU):
            rows = slice(i * BS, (i + 1) * BS)
            high = left[0, rows, :]
            total = dot(high, right[1]) + dot(left[1, rows, :], right[0]) + dot(high, right[0])
            for j in range(TAU):
                out_ref[s, i, j] = total[:, j * BS : (j + 1) * BS]

    def form_onsite():
        labels = lambda t: jnp.full((1, BS), rows_ref[t, 0], jnp.int32).astype(jnp.float32)
        block = lambda t: onsite[t]
        side = sides.at[0, 0]
        assemble(side, block, labels, block, labels)
        multiply(0, side, side)

    def parts_of(src):
        place = pick(src, at, r, c)
        block = lambda t: buf[place, t, :BS, :]
        labels = lambda t: buf[place, t, BS : BS + 1, :]
        return block, labels

    arrived, formed = set(OWN), set()
    passing = max(number for number, leg in enumerate(legs) for later in legs if leg.name in names(later.src) | {later.after})
    for number, leg in enumerate(legs):
        when(leg.gets, r, c, copies[leg.name].wait_recv)
        arrived.add(leg.name)
        begin(leg.name)
        if number == 0:
            form_onsite()
        if number < passing:
            continue
        for s in range(1, STEPS):
            for at_side, pair in enumerate((final[s][:2], final[s][2:])):
                if (s, at_side) not in formed and arrived >= names(pair[0]) | names(pair[1]):
                    assemble(sides.at[s, at_side], *parts_of(pair[0]), *parts_of(pair[1]))
                    formed.add((s, at_side))
            if s not in formed and {(s, 0), (s, 1)} <= formed:
                multiply(s, sides.at[s, 0], sides.at[s, 1])
                formed.add(s)
    for leg in legs:
        when(leg.sends, r, c, copies[leg.name].wait_send)


def shards(u_blocks, u_rows):
    legs, final = plan()
    count = len(OWN) + len(legs)
    return pl.pallas_call(
        functools.partial(kernel, legs, final),
        out_shape=pltpu.VMEM((STEPS, TAU, TAU, BS, BS), jnp.float32),
        in_specs=[pl.BlockSpec(memory_space=pltpu.HBM)] * 2,
        out_specs=pl.BlockSpec(memory_space=pltpu.VMEM),
        scratch_shapes=[
            pltpu.VMEM((count, TAU, HEIGHT, BS), jnp.float32),
            pltpu.VMEM((TAU, BS, BS), jnp.float32),
            pltpu.SMEM((TAU, 2 * STEPS - 1), jnp.int32),
            pltpu.VMEM((STEPS, 2, 2, TAU * BS, TAU * BS), jnp.bfloat16),
            pltpu.SemaphoreType.DMA,
            pltpu.SemaphoreType.DMA((2 * STEPS - 1, TAU)),
            pltpu.SemaphoreType.DMA((len(legs),)),
            pltpu.SemaphoreType.DMA((len(legs),)),
        ],
        compiler_params=pltpu.CompilerParams(collective_id=0, has_side_effects=True, vmem_limit_bytes=40 << 20),
    )(*(pltpu.with_memory_space_constraint(each, pltpu.HBM) for each in (u_blocks, u_rows)))


def solution(mesh):
    return jax.shard_map(
        shards,
        mesh=mesh,
        in_specs=(P("row", "col", None, None), P("row", "col")),
        out_specs=P("row", "col", None, None, None),
        check_vma=False,
    )
```

```python
import functools

import jax
import jax.numpy as jnp
from jax import lax
from jax.experimental import pallas as pl
from jax.experimental.pallas import tpu as pltpu
from jax.sharding import PartitionSpec as P

MESH = pl.DeviceIdType.MESH
BS = 128
TAU = 3
STEPS = 4
N_ROW = 32
N_COL = 24
HEIGHT = BS + 8

RING = 8


def straight(k, m):
    return (
        lambda r, c: ((r + N_ROW - k) % N_ROW, (c + N_COL - m) % N_COL),
        lambda r, c: ((r + N_ROW + k) % N_ROW, (c + N_COL + m) % N_COL),
    )


def around(at, k):
    return at - at % RING + (at % RING + RING - k) % RING


def in_plane(k, m):
    return lambda r, c: (around(r, k), around(c, m)), lambda r, c: (around(r, -k), around(c, -m))


def in_row_plane(k, m):
    return (
        lambda r, c: (around(r, k), (c + N_COL - m) % N_COL),
        lambda r, c: (around(r, -k), (c + m) % N_COL),
    )


def wrapped(at, k):
    return jnp.where(at % RING >= RING - k, RING, 0)


def down(k, m):
    return (
        lambda r, c: ((r + N_ROW - wrapped(r, k)) % N_ROW, (c + N_COL - wrapped(c, m)) % N_COL),
        lambda r, c: ((r + wrapped(r, k)) % N_ROW, (c + wrapped(c, m)) % N_COL),
    )


class Leg:
    def __init__(self, name, src, move, sends=None):
        self.name, self.src, self.sends, self.after = name, src, sends, AFTER.get(name)
        self.to, self.origin = move
        self.gets = None if sends is None else lambda r, c: sends(*self.origin(r, c))


def plan():
    legs, final = {}, {}

    def leg(name, src, move, sends=None):
        legs[name] = Leg(name, src, move, sends)
        return name

    def late(name, src, k, m):
        crossed = lambda r, c: (r % RING >= RING - k) | (c % RING >= RING - m)
        leg(name, src, in_plane(k, m))
        leg(name + "z", name, down(k, m), crossed)
        return crossed, name + "z", name

    low = lambda k: lambda r, c: r % RING < k
    rows = lambda a, b: lambda r, c: (r % RING >= a) & (r % RING < b)
    wide = lambda r, c: c % RING >= 4

    leg("f3", "F3", straight(RING, 0), low(6))
    leg("fe3", (low(6), "f3", "F3"), in_plane(6, 0))
    leg("fm3", (low(3), "f3", "F3"), in_row_plane(3, 3))
    bs3 = late("bs3", "B3", 0, 6)
    leg("bm3", bs3, straight(3, -3))
    final[3] = "fm3", bs3, "fe3", "bm3"

    leg("f2", "F2", straight(RING, 0), rows(2, 4))
    leg("fe2", (rows(2, 4), "f2", "F2"), in_plane(4, 0))
    leg("fe2z", "fe2", straight(RING, 0), rows(4, 6))
    leg("fm2", "F2", in_row_plane(2, 2), rows(2, 8))
    leg("fm2x", "fe2z", in_row_plane(-2, 2), rows(4, 6))
    leg("p2", "B2", in_plane(0, -2))
    leg("bs2", "p2", in_plane(0, -2))
    leg("bs2z", "bs2", down(0, 4), wide)
    bm2 = late("bm2", "B2", 2, 2)
    final[2] = (rows(6, 8), "fm2x", "fm2"), (wide, "bs2z", "bs2"), (rows(4, 6), "fe2z", "fe2"), bm2

    n1 = late("n1", "F1", 1, 0)
    c1 = leg("c1", "B1", straight(0, 1))
    fe1 = late("fe1", n1, 1, 0)
    fm1 = late("fm1", n1, 0, 1)
    leg("bm1", c1, straight(1, 0))
    leg("bs1", c1, straight(0, 1))
    final[1] = fm1, "bs1", fe1, "bm1"

    return [legs[name] for name in ORDER], final


ORDER = (
    "n1", "n1z", "p2", "fe1", "fe1z", "f3", "f2", "bs3", "fm1", "bs3z", "fe2", "fe2z", "bm2", "c1", "bs2", "fe3",
    "bm1", "fm3", "bs1", "fm2", "fm2x", "bm3", "fm1z", "bm2z", "bs2z",
)
AFTER = {"bm2": "n1", "c1": "bs3", "f2": "n1", "f3": "n1", "fe2": "n1", "fm2": "n1", "fm3": "f2", "p2": "n1"}


OWN = ["F1", "F2", "F3", "B1", "B2", "B3"]


def places(legs):
    return {name: at for at, name in enumerate(OWN + [leg.name for leg in legs])}


def pick(src, at, r, c):
    if isinstance(src, str):
        return at[src]
    condition, yes, no = src
    return jnp.where(condition(r, c), at[yes], at[no])


def names(src):
    return {src} if isinstance(src, str) else set(src[1:])


def when(condition, r, c, do):
    if condition is None:
        do()
    else:
        pl.when(condition(r, c))(do)


def split(value):
    high = value.astype(jnp.bfloat16)
    return high, (value - high.astype(jnp.float32)).astype(jnp.bfloat16)


def dot(a, b):
    return jnp.dot(a, b, preferred_element_type=jnp.float32)


def kernel(legs, final, u_ref, rows_hbm, out_ref, buf, onsite, rows_ref, sides, rows_sem, load_sem, send_sem, recv_sem):
    r, c = lax.axis_index("row"), lax.axis_index("col")
    at = places(legs)
    copies = {}
    for number, leg in enumerate(legs):
        copies[leg.name] = pltpu.make_async_remote_copy(
            src_ref=buf.at[pick(leg.src, at, r, c)],
            dst_ref=buf.at[at[leg.name]],
            send_sem=send_sem.at[number],
            recv_sem=recv_sem.at[number],
            device_id=leg.to(r, c),
            device_id_type=MESH,
        )

    barrier = pltpu.get_barrier_semaphore()
    partners = 0
    for leg in legs:
        greet = functools.partial(
            pl.semaphore_signal, barrier, inc=1, device_id=leg.origin(r, c), device_id_type=MESH
        )
        when(leg.gets, r, c, greet)
        partners += 1 if leg.sends is None else jnp.where(leg.sends(r, c), 1, 0)

    labels_load = pltpu.make_async_copy(rows_hbm, rows_ref, rows_sem)
    labels_load.start()
    loads = {}
    for j in (1, 6, 2, 3, 5, 4, 0):
        loads[j] = []
        for t in range(TAU):
            target = onsite.at[t] if j == 0 else buf.at[j - 1, t, pl.ds(0, BS)]
            loads[j].append(pltpu.make_async_copy(u_ref.at[t, j], target, load_sem.at[j, t]))
            loads[j][-1].start()
    labels_load.wait()
    for j in range(1, 2 * STEPS - 1):
        for t in range(TAU):
            buf[j - 1, t, BS:HEIGHT, :] = jnp.full((HEIGHT - BS, BS), rows_ref[t, j], jnp.int32).astype(jnp.float32)
    pl.semaphore_wait(barrier, partners)

    def loaded(j):
        for load in loads.pop(j, ()):
            load.wait()

    rank = {None: -1, **{leg.name: number for number, leg in enumerate(legs)}}

    def trigger(leg, source):
        return max(None if source in OWN else source, leg.after, key=rank.get)

    def begin(event):
        for leg in legs:
            go = copies[leg.name].start
            if event is None:
                own = leg.src if isinstance(leg.src, str) else leg.src[2]
                if own in OWN and trigger(leg, own) is None:
                    loaded(1 + OWN.index(own))
            if isinstance(leg.src, str):
                if event == trigger(leg, leg.src):
                    when(leg.sends, r, c, go)
            else:
                condition, yes, no = leg.src
                if event == trigger(leg, yes):
                    when(condition, r, c, go)
                if event == trigger(leg, no):
                    when(lambda r, c: jnp.logical_not(condition(r, c)), r, c, go)

    begin(None)
    for j in list(loads):
        loaded(j)

    def put(side, i, k, value):
        high, low = split(value)
        side[0, i * BS : (i + 1) * BS, k * BS : (k + 1) * BS] = high
        side[1, i * BS : (i + 1) * BS, k * BS : (k + 1) * BS] = low

    def chosen(label, k, block):
        return jnp.where(label == float(k), block, 0.0)

    def assemble(side, forward, forward_labels, backward, backward_labels):
        for i in range(TAU):
            turned = backward(i).T
            for k in range(TAU):
                put(side, i, k, chosen(forward_labels(k), i, forward(k)) + chosen(backward_labels(i), k, turned))

    def multiply(s, left, right):
        for i in range(TAU):
            rows = slice(i * BS, (i + 1) * BS)
            high = left[0, rows, :]
            total = dot(high, right[1]) + dot(left[1, rows, :], right[0]) + dot(high, right[0])
            for j in range(TAU):
                out_ref[s, i, j] = total[:, j * BS : (j + 1) * BS]

    def form_onsite():
        labels = lambda t: jnp.full((1, BS), rows_ref[t, 0], jnp.int32).astype(jnp.float32)
        block = lambda t: onsite[t]
        side = sides.at[0, 0]
        assemble(side, block, labels, block, labels)
        multiply(0, side, side)

    def parts_of(src):
        place = pick(src, at, r, c)
        block = lambda t: buf[place, t, :BS, :]
        labels = lambda t: buf[place, t, BS : BS + 1, :]
        return block, labels

    arrived, formed = set(OWN), set()
    passing = max(number for number, leg in enumerate(legs) for later in legs if leg.name in names(later.src) | {later.after})
    for number, leg in enumerate(legs):
        when(leg.gets, r, c, copies[leg.name].wait_recv)
        arrived.add(leg.name)
        begin(leg.name)
        if number == 0:
            form_onsite()
        if number < passing:
            continue
        for s in range(1, STEPS):
            for at_side, pair in enumerate((final[s][:2], final[s][2:])):
                if (s, at_side) not in formed and arrived >= names(pair[0]) | names(pair[1]):
                    assemble(sides.at[s, at_side], *parts_of(pair[0]), *parts_of(pair[1]))
                    formed.add((s, at_side))
            if s not in formed and {(s, 0), (s, 1)} <= formed:
                multiply(s, sides.at[s, 0], sides.at[s, 1])
                formed.add(s)
    for leg in legs:
        when(leg.sends, r, c, copies[leg.name].wait_send)


def shards(u_blocks, u_rows):
    legs, final = plan()
    count = len(OWN) + len(legs)
    return pl.pallas_call(
        functools.partial(kernel, legs, final),
        out_shape=pltpu.VMEM((STEPS, TAU, TAU, BS, BS), jnp.float32),
        in_specs=[pl.BlockSpec(memory_space=pltpu.HBM)] * 2,
        out_specs=pl.BlockSpec(memory_space=pltpu.VMEM),
        scratch_shapes=[
            pltpu.VMEM((count, TAU, HEIGHT, BS), jnp.float32),
            pltpu.VMEM((TAU, BS, BS), jnp.float32),
            pltpu.SMEM((TAU, 2 * STEPS - 1), jnp.int32),
            pltpu.VMEM((STEPS, 2, 2, TAU * BS, TAU * BS), jnp.bfloat16),
            pltpu.SemaphoreType.DMA,
            pltpu.SemaphoreType.DMA((2 * STEPS - 1, TAU)),
            pltpu.SemaphoreType.DMA((len(legs),)),
            pltpu.SemaphoreType.DMA((len(legs),)),
        ],
        compiler_params=pltpu.CompilerParams(collective_id=0, has_side_effects=True, vmem_limit_bytes=40 << 20),
    )(*(pltpu.with_memory_space_constraint(each, pltpu.HBM) for each in (u_blocks, u_rows)))


def solution(mesh):
    return jax.shard_map(
        shards,
        mesh=mesh,
        in_specs=(P("row", "col", None, None), P("row", "col")),
        out_specs=P("row", "col", None, None, None),
        check_vma=False,
    )
```
